128 devices in a mesh: farm: 16 (over x_hi, z, core), fsdp: 8 (over y, x_lo).
Axes of the slice: x: 4 (x_hi: 2, x_lo: 2; x = x_hi * 2 + x_lo), y: 4, z: 4, core: 2. Of those that a mesh axis runs over, the one named last changes fastest.
Arguments:
- activations: bfloat16 [16, 4096, 8192], P('farm', 'fsdp'), may hold values from -6 to 6
- out_grads: bfloat16 [16, 4096, 512], P('farm', 'fsdp'), may hold values from -6 to 6
- weights: float32 [16, 8192, 512], P('farm', 'fsdp'), may hold values from -6 to 6
- anchor: float32 [16, 8192, 512], P('farm', 'fsdp'), may hold values from -6 to 6
- adam_m: float32 [16, 8192, 512], P('farm', 'fsdp'), may hold values from -0.25 to 0.25
- adam_v: float32 [16, 8192, 512], P('farm', 'fsdp'), may hold values from 2.4414063e-05 to 0.0024414062
- momentum: float32 [16, 8192, 512], P('farm', 'fsdp'), may hold values from -6 to 6
- partner: int32 [16], replicated, may hold values from 0 to 15, as said below
Outputs:
- new_anchor: float32 [16, 8192, 512], P('farm', 'fsdp')
- new_momentum: float32 [16, 8192, 512], P('farm', 'fsdp')
The draws below stay inside these ranges and needn't reach their ends.
Inputs may be any that keep to these rules, and one draw needn't show every extreme that they name: partner is a perfect matching of the 16 farms: partner[partner[f]] = f and partner[f] != f.
All inputs are finite; a program needn't handle non-finite values.
Results may differ from the reference program's by a relative error of at most 0.0003.
Values sent between devices are 32-bit elements; how exact they have to be, the bound alone decides.
A program may use at most 128 MiB of HBM per device.

```python
import math
import jax
import jax.numpy as jnp
from jax import lax

D = 8192
KV = 512
TOK_DEV = 512
FTOK = 4096
FARMS = 16
N_FSDP = 8


def draw_partner(key, part):
    key = jax.random.fold_in(key, 7)
    farm_order = jax.random.permutation(key, FARMS).astype(jnp.int32)
    swapped = farm_order.reshape(FARMS // 2, 2)[:, ::-1].reshape(FARMS)
    return jnp.zeros((FARMS,), jnp.int32).at[farm_order].set(swapped)


def spiked(drawn, stream_key, source, target, blocks, factor):
    owner, partner = [(jnp.arange(drawn.shape[dim]) // (drawn.shape[dim] // blocks)).reshape([-1 if axis == dim else 1 for axis in range(drawn.ndim)]) for dim in (source, target)]
    chosen = jax.random.permutation(stream_key, blocks)[partner]
    strong = (owner == chosen) | (owner == (partner + blocks // 2) % blocks)
    return jnp.where(strong, factor * drawn, drawn)


def level_of(key, shape, pieces, smallest, largest):
    def one(axis_at, shards_of):
        steps = jax.random.uniform(jax.random.fold_in(jax.random.fold_in(key, 6), axis_at), (shards_of,), jnp.float32, smallest / len(pieces), largest / len(pieces))
        return jnp.repeat(jnp.exp(steps), shape[axis_at] // shards_of).reshape((-1,) + (1,) * (len(shape) - axis_at - 1))

    gain = one(*pieces[0])
    for cut in pieces[1:]:
        gain = gain * one(*cut)
    return gain


def noise(key, dims, width, reach, cuts=(), kind=jnp.bfloat16):
    entries = width * jax.random.normal(key, dims, jnp.float32)
    if cuts:
        entries = entries * level_of(key, dims, cuts, -0.22, 0.18)
    return jnp.clip(entries, -reach, reach).astype(kind)


def bell_draw_with(key, shape, deviation, most, shards, heavy, dtype=jnp.bfloat16):
    result = deviation * jax.random.normal(key, shape, jnp.float32)
    if shards:
        result = result * level_of(key, shape, shards, -0.22, 0.18)
    return jnp.clip(spiked(result, jax.random.fold_in(key, 3), *heavy), -most, most).astype(dtype)


def setup_inputs(seed: int = 0) -> dict:
    arg_keys = jax.random.split(jax.random.key(seed), 9)
    activations = bell_draw_with(arg_keys[0], (FARMS, FTOK, D), 1.0, 6.0, ((0, 16), (1, 8)), (1, 2, 8, 2.0))
    out_grads = noise(arg_keys[1], (FARMS, FTOK, KV), 1.0, 6.0, ((0, 16), (1, 8)))
    weights = noise(arg_keys[2], (FARMS, D, KV), 0.5, 6.0, ((0, 16), (1, 8)), jnp.float32)
    anchor = noise(arg_keys[3], (FARMS, D, KV), 0.5, 6.0, ((0, 16), (1, 8)), jnp.float32)
    adam_m = noise(arg_keys[4], (FARMS, D, KV), (FTOK ** -0.5), 0.25, ((0, 16), (1, 8)), jnp.float32)
    adam_v = jnp.clip(jnp.exp(math.log(0.0024414062) - 4.6051702 * jax.random.uniform(arg_keys[5], (FARMS, D, KV), jnp.float32) ** level_of(arg_keys[5], (FARMS, D, KV), ((0, 16), (1, 8)), -0.2, 0.2)), 2.441406286379788e-05, 0.0024414062)
    momentum = noise(arg_keys[6], (FARMS, D, KV), 0.5, 6.0, ((0, 16), (1, 8)), jnp.float32)
    partner = draw_partner(jax.random.fold_in(arg_keys[8], 71), 0)
    return {"activations": activations, "out_grads": out_grads, "weights": weights, "anchor": anchor, "adam_m": adam_m, "adam_v": adam_v, "momentum": momentum, "partner": partner}


def farm_gradient(pair):
    acts, grads = pair
    acts = acts.reshape(N_FSDP, TOK_DEV, D)
    grads = grads.reshape(N_FSDP, TOK_DEV, KV)

    def add_block(total, block):
        term = lax.dot_general(block[0], block[1], (((0,), (0,)), ((), ())), preferred_element_type=jnp.float32)
        return (total + term, None)
    total, unused = lax.scan(add_block, jnp.zeros((D, KV), jnp.float32), (acts, grads))
    return total

def reference(activations, out_grads, weights, anchor, adam_m, adam_v, momentum, partner):
    gradient = lax.map(farm_gradient, (activations, out_grads)) / FTOK
    first_moment = 0.9 * adam_m + 0.1 * gradient
    second_moment = 0.95 * adam_v + 0.05 * gradient * gradient
    inner = weights - 0.3 * (first_moment / (jnp.sqrt(second_moment) + 1e-08) + 0.1 * weights)
    delta = anchor - inner
    mean_delta = 0.5 * delta + 0.5 * jnp.take(delta, partner, axis=0)
    mean_momentum = 0.5 * momentum + 0.5 * jnp.take(momentum, partner, axis=0)
    mean_anchor = 0.5 * anchor + 0.5 * jnp.take(anchor, partner, axis=0)
    new_momentum = 0.9 * mean_momentum + mean_delta
    new_anchor = mean_anchor - 0.7 * (0.9 * new_momentum + mean_delta)
    return (new_anchor, new_momentum)
```

```python
import functools

import jax
import jax.numpy as jnp
from jax import lax
from jax.experimental import pallas as pl
from jax.experimental.pallas import tpu as pltpu
from jax.sharding import PartitionSpec as P

MESH = pl.DeviceIdType.MESH
FARMS = 16
YS = 4
ROWS = 128
CW = 256
SLOTS = 4
PIECE = ROWS // FARMS
E_FIRST, E_PER = 0, 4
E_BLEND, E_BACK_PER = 6, 2


def kernel(
    partner, acts, grads, weights, anchor, adam_m, adam_v, momentum,
    mean_nm, mean_e,
    acts_v, grads_v, state, part, got_y, got_x, mine, got_f, pieces, blended, early, got_e, blended_e,
    load_a, load_s, y_send, y_recv, x_send, x_recv, f_send, f_recv, b_send, b_recv, e_sems, own_sem,
):
    shard = weights.shape[0]
    width = weights.shape[1]
    tokens = acts.shape[0]
    col_blocks = width // CW
    row_blocks = shard // ROWS
    chunks = row_blocks * col_blocks
    e_rows = shard // FARMS

    me = lax.axis_index("farm")
    place = lax.axis_index("fsdp")
    y, half = place // 2, lax.rem(place, 2)
    y_up, y_op, y_dn = lax.rem(y + 1, YS), lax.rem(y + 2, YS), lax.rem(y + 3, YS)
    up = {"fsdp": y_up * 2 + half}
    dn = {"fsdp": y_dn * 2 + half}
    side = {"fsdp": y * 2 + (1 - half)}

    def farm(i):
        return {"farm": lax.rem(me + i, FARMS)}

    barrier = pltpu.get_barrier_semaphore()
    for other in (up, dn, side):
        pl.semaphore_signal(barrier, inc=1, device_id=other, device_id_type=MESH)
    for i in range(1, FARMS):
        pl.semaphore_signal(barrier, inc=1, device_id=farm(i), device_id_type=MESH)

    def load_acts(block):
        for s in range(2 * YS):
            pltpu.make_async_copy(
                acts.at[:, pl.ds(s * shard + block * ROWS, ROWS)], acts_v.at[block, s], load_a.at[block]
            ).start()

    def load_state(n, ref):
        for c in range(col_blocks):
            pltpu.make_async_copy(ref.at[:, pl.ds(c * CW, CW)], state.at[n, c], load_s.at[n]).start()

    for c in range(col_blocks):
        pltpu.make_async_copy(grads.at[:, pl.ds(c * CW, CW)], grads_v.at[c], load_s.at[5]).start()
    load_acts(0)
    load_state(0, anchor)
    load_state(1, momentum)
    for block in range(1, row_blocks):
        load_acts(block)
    load_state(2, weights)
    load_state(3, adam_m)
    load_state(4, adam_v)

    def wait_bytes(ref, sem):
        pltpu.make_async_copy(ref, ref, sem).wait()

    def y_copy(k, slot, i, to, j):
        return pltpu.make_async_remote_copy(
            src_ref=part.at[slot, i], dst_ref=got_y.at[k, j], send_sem=y_send.at[slot, j], recv_sem=y_recv.at[k, j],
            device_id=to, device_id_type=MESH,
        )

    def x_copy(k, slot):
        return pltpu.make_async_remote_copy(
            src_ref=part.at[slot, 7 - half], dst_ref=got_x.at[k], send_sem=x_send.at[slot], recv_sem=x_recv.at[k],
            device_id=side, device_id_type=MESH,
        )

    def wait_y(k, j):
        wait_bytes(got_y.at[k, j], y_recv.at[k, j])

    def wait_sent(slot):
        for j in range(6):
            wait_bytes(part.at[slot, 0], y_send.at[slot, j])
        wait_bytes(part.at[slot, 0], x_send.at[slot])

    wait_bytes(grads_v, load_s.at[5])

    def multiply(k):
        slot, block, c = lax.rem(k, SLOTS), k // col_blocks, lax.rem(k, col_blocks)

        @pl.when(c == 0)
        def _():
            wait_bytes(acts_v.at[block], load_a.at[block])

        @pl.when(k >= SLOTS)
        def _():
            wait_sent(slot)

        cot = grads_v[c]
        for i, (yd, h) in enumerate(((y_op, 0), (y_op, 1), (y_dn, 0), (y_up, 1), (y_up, 0), (y_dn, 1), (y, 0), (y, 1))):
            part[slot, i] = lax.dot_general(
                acts_v[block, yd * 2 + h], cot, (((0,), (0,)), ((), ())), preferred_element_type=jnp.float32
            )
            if i == 1:

                @pl.when(k == 0)
                def _():
                    pl.semaphore_wait(barrier, 3 + FARMS - 1)

                y_copy(k, slot, 0, up, 0).start()
                y_copy(k, slot, 1, dn, 1).start()
            if i == 2:
                y_copy(k, slot, 2, dn, 2).start()
            if i == 3:
                y_copy(k, slot, 3, up, 3).start()

    def pass_on(k):
        slot = lax.rem(k, SLOTS)
        for h, to in ((0, up), (1, dn)):
            wait_y(k, h)
            part[slot, 4 + h] += got_y[k, h]
            y_copy(k, slot, 4 + h, to, 4 + h).start()

    def finish_y(k):
        slot = lax.rem(k, SLOTS)
        for h in (1 - half, half):
            wait_y(k, 2 + h)
            wait_y(k, 4 + h)
            part[slot, 6 + h] += got_y[k, 2 + h] + got_y[k, 4 + h]
            if h is not half:
                x_copy(k, slot).start()

    def update(k):
        slot, block, c = lax.rem(k, SLOTS), k // col_blocks, lax.rem(k, col_blocks)

        @pl.when(k == 0)
        def _():
            for n in (2, 3, 4):
                wait_bytes(state.at[n], load_s.at[n])

        rows = pl.ds(pl.multiple_of(block * ROWS, ROWS), ROWS)
        wait_bytes(got_x.at[k], x_recv.at[k])
        gradient = (part[slot, 6 + half] + got_x[k]) * (1.0 / (tokens * 2 * YS))
        anchor_c, mom_c, w_c = state[0, c, rows], state[1, c, rows], state[2, c, rows]
        m1 = 0.9 * state[3, c, rows] + 0.1 * gradient
        v1 = 0.95 * state[4, c, rows] + 0.05 * gradient * gradient
        inner = w_c - 0.3 * (m1 / (jnp.sqrt(v1) + 1e-08) + 0.1 * w_c)
        mine[k] = 0.9 * mom_c + (anchor_c - inner)
        got_f[k, me] = mine[k, pl.ds(pl.multiple_of(me * PIECE, PIECE), PIECE)]

        def send(i, carry):
            to = lax.rem(me + i, FARMS)
            pltpu.make_async_remote_copy(
                src_ref=mine.at[k, pl.ds(pl.multiple_of(to * PIECE, PIECE), PIECE)], dst_ref=got_f.at[k, me],
                send_sem=f_send.at[k], recv_sem=f_recv.at[k], device_id={"farm": to}, device_id_type=MESH,
            ).start()
            return carry

        lax.fori_loop(1, FARMS, send, 0)

    def nm_rows(k, owner):
        block, c = k // col_blocks, lax.rem(k, col_blocks)
        return (
            pl.ds(pl.multiple_of(block * ROWS + owner * PIECE, PIECE), PIECE),
            pl.ds(pl.multiple_of(c * CW, CW), CW),
        )

    def average(k):
        wait_bytes(got_f.at[k, pl.ds(0, FARMS - 1)], f_recv.at[k])

        pieces[...] = got_f[k]

        def blend(f, carry):
            blended[k, f] = 0.5 * (pieces[f] + pieces[partner[f]])
            return carry

        lax.fori_loop(0, FARMS, blend, 0)
        pltpu.make_async_copy(blended.at[k, me], mean_nm.at[nm_rows(k, me)], own_sem.at[k]).start()

        def send(i, carry):
            to = lax.rem(me + i, FARMS)
            pltpu.make_async_remote_copy(
                src_ref=blended.at[k, to], dst_ref=mean_nm.at[nm_rows(k, me)],
                send_sem=b_send.at[k], recv_sem=b_recv.at[k], device_id={"farm": to}, device_id_type=MESH,
            ).start()
            return carry

        lax.fori_loop(1, FARMS, send, 0)

    def e_piece(owner):
        return pl.ds(pl.multiple_of(owner * e_rows, e_rows), e_rows)

    def make_early():
        for n in (0, 1):
            wait_bytes(state.at[n], load_s.at[n])

        def block_of(b, carry):
            rows = pl.ds(pl.multiple_of(b * ROWS, ROWS), ROWS)
            for c in range(col_blocks):
                early[rows, pl.ds(c * CW, CW)] = state[0, c, rows] + 0.63 * state[1, c, rows]
            return carry

        lax.fori_loop(0, row_blocks, block_of, 0)
        got_e[me] = early[e_piece(me)]

    def send_early(first):
        def send(i, carry):
            to = lax.rem(me + i, FARMS)
            pltpu.make_async_remote_copy(
                src_ref=early.at[e_piece(to)], dst_ref=got_e.at[me],
                send_sem=e_sems.at[0], recv_sem=e_sems.at[1], device_id={"farm": to}, device_id_type=MESH,
            ).start()
            return carry

        lax.fori_loop(first, jnp.minimum(first + E_PER, FARMS), send, 0)

    def average_early():
        wait_bytes(got_e.at[pl.ds(0, FARMS - 1)], e_sems.at[1])

        def blend(f, carry):
            blended_e[f] = 0.5 * (got_e[f] + got_e[partner[f]])
            return carry

        lax.fori_loop(0, FARMS, blend, 0)
        pltpu.make_async_copy(blended_e.at[me], mean_e.at[e_piece(me)], own_sem.at[chunks]).start()

    def return_early(first):
        def send(i, carry):
            to = lax.rem(me + i, FARMS)
            pltpu.make_async_remote_copy(
                src_ref=blended_e.at[to], dst_ref=mean_e.at[e_piece(me)],
                send_sem=e_sems.at[2], recv_sem=e_sems.at[3], device_id={"farm": to}, device_id_type=MESH,
            ).start()
            return carry

        lax.fori_loop(first, jnp.minimum(first + E_BACK_PER, FARMS), send, 0)

    out_steps = -(-(FARMS - 1) // E_PER)
    back_steps = -(-(FARMS - 1) // E_BACK_PER)

    def step(t, carry):
        pl.when(t < chunks)(lambda: multiply(t))
        pl.when(t == E_FIRST)(make_early)
        pl.when((t >= E_FIRST) & (t < E_FIRST + out_steps))(lambda: send_early((t - E_FIRST) * E_PER + 1))
        pl.when((t >= 1) & (t < chunks + 1))(lambda: pass_on(t - 1))
        pl.when((t >= 2) & (t < chunks + 2))(lambda: finish_y(t - 2))
        pl.when((t >= 3) & (t < chunks + 3))(lambda: update(t - 3))
        pl.when((t >= 4) & (t < chunks + 4))(lambda: average(t - 4))
        pl.when(t == E_BLEND)(average_early)
        pl.when((t >= E_BLEND) & (t < E_BLEND + back_steps))(lambda: return_early((t - E_BLEND) * E_BACK_PER + 1))
        return carry

    lax.fori_loop(0, chunks + 4, step, 0)

    for slot in range(SLOTS):
        wait_sent(slot)
    for sem in (e_sems.at[0], e_sems.at[2], e_sems.at[3]):
        wait_bytes(got_e.at[pl.ds(0, FARMS - 1)], sem)
    wait_bytes(blended_e.at[0], own_sem.at[chunks])

    def last(k, carry):
        wait_bytes(blended.at[k, 0], own_sem.at[k])
        for sem in (f_send.at[k], b_send.at[k], b_recv.at[k]):
            wait_bytes(got_f.at[k, pl.ds(0, FARMS - 1)], sem)
        return carry

    lax.fori_loop(0, chunks, last, 0)


def on_device(activations, out_grads, weights, anchor, adam_m, adam_v, momentum, partner):
    tokens = activations.shape[1]
    shard, width = weights.shape[1:]
    col_blocks, row_blocks = width // CW, shard // ROWS
    chunks = col_blocks * row_blocks
    e_rows = shard // FARMS
    f32 = jnp.float32
    dma = pltpu.SemaphoreType.DMA
    anywhere = pl.BlockSpec(memory_space=pl.ANY)
    mean_nm, mean_e = pl.pallas_call(
        kernel,
        out_shape=[jax.ShapeDtypeStruct((shard, width), f32)] * 2,
        in_specs=[pl.BlockSpec(memory_space=pltpu.SMEM)] + [anywhere] * 7,
        out_specs=[anywhere] * 2,
        scratch_shapes=[
            pltpu.VMEM((row_blocks, 2 * YS, tokens, ROWS), jnp.bfloat16),
            pltpu.VMEM((col_blocks, tokens, CW), jnp.bfloat16),
            pltpu.VMEM((5, col_blocks, shard, CW), f32),
            pltpu.VMEM((SLOTS, 8, ROWS, CW), f32),
            pltpu.VMEM((chunks, 6, ROWS, CW), f32),
            pltpu.VMEM((chunks, ROWS, CW), f32),
            pltpu.VMEM((chunks, ROWS, CW), f32),
            pltpu.VMEM((chunks, FARMS, PIECE, CW), f32),
            pltpu.VMEM((FARMS, PIECE, CW), f32),
            pltpu.VMEM((chunks, FARMS, PIECE, CW), f32),
            pltpu.VMEM((shard, width), f32),
            pltpu.VMEM((FARMS, e_rows, width), f32),
            pltpu.VMEM((FARMS, e_rows, width), f32),
            dma((row_blocks,)),
            dma((6,)),
            dma((SLOTS, 6)),
            dma((chunks, 6)),
            dma((SLOTS,)),
            dma((chunks,)),
            dma((chunks,)),
            dma((chunks,)),
            dma((chunks,)),
            dma((chunks,)),
            dma((4,)),
            dma((chunks + 1,)),
        ],
        compiler_params=pltpu.CompilerParams(
            collective_id=0, has_side_effects=True, vmem_limit_bytes=60 << 20
        ),
        cost_estimate=pl.CostEstimate(
            flops=2 * tokens * 2 * YS * shard * width, bytes_accessed=24 << 20, transcendentals=shard * width
        ),
        name="outer_step",
    )(partner, activations[0], out_grads[0], weights[0], anchor[0], adam_m[0], adam_v[0], momentum[0])
    new_anchor = mean_e - 1.33 * mean_nm
    return new_anchor[None], mean_nm[None]


def solution(mesh):
    split = P("farm", "fsdp", None)
    return jax.shard_map(
        on_device, mesh=mesh, in_specs=(split,) * 7 + (P(),), out_specs=(split, split), check_vma=False
    )
```

```python
import functools
from typing import NamedTuple

import jax
import jax.numpy as jnp
from jax import lax
from jax.experimental import pallas as pl
from jax.experimental.pallas import tpu as pltpu
from jax.sharding import PartitionSpec as P

MESH = pl.DeviceIdType.MESH
FARMS = 16
YS = 4
ROWS = 128
CW = 256
SLOTS = 4
SIDE = 8
PIECE = ROWS // SIDE
WIDE_LAG = 2


class Plan(NamedTuple):
    number: int
    crossing: int
    direct: int
    wide_chunks: int
    wide_steps: tuple
    early_per: int
    early_cross: int
    update_lag: int
    update_catch: tuple
    average_lag: int
    average_catch: tuple


def kernel(
    plan,
    partner, acts, grads, weights, anchor, adam_m, adam_v, momentum,
    new_momentum, new_anchor,
    acts_v, grads_v, state, part, got_y, got_x, mine, got_f, to_cross, got_c, pieces, blended,
    got_d, early, got_e, e_to_cross, got_ec, e_pieces, wide, wide_side, wide_sum, wide_y, order,
    load_a, load_s, y_send, y_recv, x_send, x_recv, f_send, f_recv, c_send, c_recv, d_send, d_recv, b_send, b_recv, own_sem,
    e_send, e_recv, ec_send, ec_recv, w_send, w_recv, wy_send, wy_recv,
):
    shard = weights.shape[0]
    width = weights.shape[1]
    tokens = acts.shape[0]
    col_blocks = width // CW
    row_blocks = shard // ROWS
    chunks = row_blocks * col_blocks
    crossing, wide_chunks = plan.crossing, plan.wide_chunks
    first_direct = chunks - plan.direct
    y_chunks = chunks - wide_chunks
    half_cw = CW // 2
    wide_block = y_chunks // col_blocks

    me = lax.axis_index("farm")
    place = lax.axis_index("fsdp")
    y, half = place // 2, lax.rem(place, 2)
    y_up, y_op, y_dn = lax.rem(y + 1, YS), lax.rem(y + 2, YS), lax.rem(y + 3, YS)
    up = {"fsdp": y_up * 2 + half}
    dn = {"fsdp": y_dn * 2 + half}
    side = {"fsdp": y * 2 + (1 - half)}
    base = me // SIDE * SIDE
    seat = me - base
    across = SIDE - base
    mirror = {"farm": across + seat}

    def seat_at(i):
        return lax.rem(seat + i, SIDE)

    barrier = pltpu.get_barrier_semaphore()
    for other in (up, dn, side):
        pl.semaphore_signal(barrier, inc=1, device_id=other, device_id_type=MESH)
    for i in range(1, SIDE):
        pl.semaphore_signal(barrier, inc=1, device_id={"farm": base + seat_at(i)}, device_id_type=MESH)
    for i in range(SIDE):
        pl.semaphore_signal(barrier, inc=1, device_id={"farm": across + seat_at(i)}, device_id_type=MESH)

    def load_acts(block):
        for s in range(2 * YS):
            pltpu.make_async_copy(
                acts.at[:, pl.ds(s * shard + block * ROWS, ROWS)], acts_v.at[block, s], load_a.at[block]
            ).start()

    def load_state(n, ref):
        for c in range(col_blocks):
            pltpu.make_async_copy(ref.at[:, pl.ds(c * CW, CW)], state.at[n, c], load_s.at[n]).start()

    def load_rest():
        load_state(0, anchor)
        load_state(1, momentum)
        for block in (*range(wide_block, row_blocks), *range(1, wide_block)):
            load_acts(block)
        load_state(2, weights)
        load_state(3, adam_m)
        load_state(4, adam_v)

    for c in range(col_blocks):
        pltpu.make_async_copy(grads.at[:, pl.ds(c * CW, CW)], grads_v.at[c], load_s.at[5]).start()
    load_acts(0)

    def wait_bytes(ref, sem):
        pltpu.make_async_copy(ref, ref, sem).wait()

    def remote(src, dst, send, recv, to):
        pltpu.make_async_remote_copy(
            src_ref=src, dst_ref=dst, send_sem=send, recv_sem=recv, device_id=to, device_id_type=MESH
        ).start()

    def product(block, s, cot):
        return lax.dot_general(acts_v[block, s], cot, (((0,), (0,)), ((), ())), preferred_element_type=jnp.float32)

    def wait_sent(slot):
        for j in range(6):
            wait_bytes(part.at[slot, 0], y_send.at[slot, j])
        wait_bytes(part.at[slot, 0], x_send.at[slot])

    wait_bytes(grads_v, load_s.at[5])

    def multiply(k):
        slot, block, c = lax.rem(k, SLOTS), k // col_blocks, lax.rem(k, col_blocks)

        @pl.when((c == 0) & (block < wide_block))
        def _():
            wait_bytes(acts_v.at[block], load_a.at[block])

        @pl.when(k >= SLOTS)
        def _():
            wait_sent(slot)

        def send(i, to):
            remote(part.at[slot, i], got_y.at[k, i], y_send.at[slot, i], y_recv.at[k, i], to)

        cot = grads_v[c]
        for i, (yd, h) in enumerate(((y_op, 0), (y_op, 1), (y_dn, 0), (y_up, 1), (y_up, 0), (y_dn, 1), (y, 0), (y, 1))):
            part[slot, i] = product(block, yd * 2 + h, cot)
            if i == 1:

                @pl.when(k == 0)
                def _():
                    pl.semaphore_wait(barrier, 3 + FARMS - 1)

                send(0, up)
                send(1, dn)
            if i == 2:
                send(2, dn)
            if i == 3:
                send(3, up)

    def pass_on(k):
        slot = lax.rem(k, SLOTS)
        for h, to in ((0, up), (1, dn)):
            wait_bytes(got_y.at[k, h], y_recv.at[k, h])
            i = 4 + h
            part[slot, i] += got_y[k, h]
            remote(part.at[slot, i], got_y.at[k, i], y_send.at[slot, i], y_recv.at[k, i], to)

    def finish_y(k):
        slot = lax.rem(k, SLOTS)
        for n, h in enumerate((1 - half, half)):
            wait_bytes(got_y.at[k, 2 + h], y_recv.at[k, 2 + h])
            wait_bytes(got_y.at[k, 4 + h], y_recv.at[k, 4 + h])
            part[slot, 6 + h] += got_y[k, 2 + h] + got_y[k, 4 + h]
            if n == 0:
                remote(part.at[slot, 6 + h], got_x.at[k], x_send.at[slot], x_recv.at[k], side)

    def gradient_of(k):
        wait_bytes(got_x.at[k], x_recv.at[k])
        return part[lax.rem(k, SLOTS), 6 + half] + got_x[k]

    def wide_part(m):
        q, d = m // YS, lax.rem(m, YS)
        k = y_chunks + q
        block, c = k // col_blocks, lax.rem(k, col_blocks)

        @pl.when(m == 0)
        def _():
            for b in range(wide_block, row_blocks):
                wait_bytes(acts_v.at[b], load_a.at[b])

        cot = grads_v[c]
        yd = lax.rem(y + d, YS)
        for h, to in ((1 - half, wide_side), (half, wide)):
            term = product(block, yd * 2 + h, cot)
            for n in range(2):
                to[q, d, n] = term[:, n * half_cw : (n + 1) * half_cw]
        remote(wide_side.at[q, d], wide_sum.at[q, d], w_send, w_recv, side)

    def wide_start(k):
        q = k - y_chunks

        @pl.when(q == 0)
        def _():
            wait_bytes(wide_sum, w_recv)

        def send(i, d, n, to):
            remote(wide.at[q, d, n], wide_y.at[q, i], wy_send.at[q, i], wy_recv.at[q, i], to)

        wide[q, 2] += wide_sum[q, 2]
        send(0, 2, 0, up)
        send(1, 2, 1, dn)
        wide[q, 1] += wide_sum[q, 1]
        wide[q, 3] += wide_sum[q, 3]
        send(2, 3, 0, dn)
        send(3, 1, 1, up)
        wide[q, 0] += wide_sum[q, 0]

    def wide_pass_on(k):
        q = k - y_chunks
        for n, to, d in ((0, up, 1), (1, dn, 3)):
            wait_bytes(wide_y.at[q, n], wy_recv.at[q, n])
            i = 4 + n
            wide[q, d, n] += wide_y[q, n]
            remote(wide.at[q, d, n], wide_y.at[q, i], wy_send.at[q, i], wy_recv.at[q, i], to)

    def wide_gradient_of(k):
        q = k - y_chunks
        halves = []
        for n in range(2):
            for i in (2 + n, 4 + n):
                wait_bytes(wide_y.at[q, i], wy_recv.at[q, i])
            halves.append(wide[q, 0, n] + wide_y[q, 2 + n] + wide_y[q, 4 + n])
        return jnp.concatenate(halves, axis=1)

    def update(k, gradient_sum):
        block, c = k // col_blocks, lax.rem(k, col_blocks)

        @pl.when(k == 0)
        def _():
            for n in (2, 3, 4):
                wait_bytes(state.at[n], load_s.at[n])

        rows = pl.ds(pl.multiple_of(block * ROWS, ROWS), ROWS)
        gradient = gradient_sum(k) * (1.0 / (tokens * 2 * YS))
        anchor_c, mom_c, w_c = state[0, c, rows], state[1, c, rows], state[2, c, rows]
        m1 = 0.9 * state[3, c, rows] + 0.1 * gradient
        v1 = 0.95 * state[4, c, rows] + 0.05 * gradient * gradient
        inner = w_c - 0.3 * (m1 / (jnp.sqrt(v1) + 1e-08) + 0.1 * w_c)
        mine[k] = 0.9 * mom_c + (anchor_c - inner)
        got_f[k, seat] = mine[k, pl.ds(pl.multiple_of(seat * PIECE, PIECE), PIECE)]

        def piece(to):
            return mine.at[k, pl.ds(pl.multiple_of(to * PIECE, PIECE), PIECE)]

        @pl.when(k >= first_direct)
        def _():
            def send_across(i, carry):
                to, q = seat_at(i), k - first_direct
                remote(piece(to), got_d.at[q, seat], d_send.at[q], d_recv.at[q], {"farm": across + to})
                return carry

            lax.fori_loop(0, SIDE, send_across, 0)

        def send(i, carry):
            to = seat_at(i)
            remote(piece(to), got_f.at[k, seat], f_send.at[k], f_recv.at[k], {"farm": base + to})
            return carry

        lax.fori_loop(1, SIDE, send, 0)

    def make_order():
        crosses = [
            [((partner[h * SIDE + g] >= SIDE) != (h == 1)).astype(jnp.int32) for g in range(SIDE)] for h in range(2)
        ]
        ranks = []
        for flags in crosses:
            total, rank = jnp.int32(0), []
            for flag in flags:
                rank.append(total)
                total = total + flag
            ranks.append(rank)
        low = base == 0
        flags = [jnp.where(low, a, b) for a, b in zip(*crosses)]
        rank = [jnp.where(low, a, b) for a, b in zip(*ranks)]
        rank_there = [jnp.where(low, b, a) for a, b in zip(*ranks)]
        for f in range(SIDE):
            p = partner[base + f]
            seat_p = jnp.where(p >= SIDE, p - SIDE, p)
            order[f] = jnp.where(flags[f] == 1, SIDE, 0) + seat_p
            there = jnp.int32(0)
            for g in range(SIDE):
                there = there + jnp.where(seat_p == g, rank_there[g], 0)
            order[SIDE + f] = jnp.where(flags[f] == 1, SIDE + there, seat_p)
        for q in range(crossing):
            farm = jnp.int32(0)
            for g in range(SIDE):
                farm = farm + jnp.where(rank[g] == q, flags[g] * g, 0)
            order[2 * SIDE + q] = farm

    def cross(k):
        wait_bytes(got_f.at[k, pl.ds(0, SIDE - 1)], f_recv.at[k])
        pieces[pl.ds(0, SIDE)] = got_f[k]
        for q in range(crossing):
            to_cross[k, q] = pieces[order[2 * SIDE + q]]
        remote(to_cross.at[k], got_c.at[k], c_send.at[k], c_recv.at[k], mirror)

    def wait_blended(slot):
        for n in range(2):
            wait_bytes(blended.at[slot, n, pl.ds(0, SIDE - 1)], b_send.at[slot, n])
            wait_bytes(blended.at[slot, n, 0], own_sem.at[slot, n])

    def average(k):
        slot, block, c = lax.rem(k, SLOTS), k // col_blocks, lax.rem(k, col_blocks)

        if crossing:

            @pl.when(c == 0)
            def _():
                wait_bytes(got_ec.at[block], ec_recv.at[block])
                e_pieces[pl.ds(0, SIDE)] = got_e[:, block]
                e_pieces[pl.ds(SIDE, crossing)] = got_ec[block]

        else:

            @pl.when(k == 0)
            def _():
                wait_bytes(got_e.at[pl.ds(0, FARMS - 1)], e_recv)

        @pl.when(k >= SLOTS)
        def _():
            wait_blended(slot)

        if crossing:

            @pl.when(k < first_direct)
            def _():
                wait_bytes(got_c.at[k], c_recv.at[k])
                pieces[pl.ds(0, SIDE)] = got_f[k]
                pieces[pl.ds(SIDE, crossing)] = got_c[k]

        @pl.when(k >= first_direct)
        def _():
            q = k - first_direct
            wait_bytes(got_f.at[k, pl.ds(0, SIDE - 1)], f_recv.at[k])
            wait_bytes(got_d.at[q], d_recv.at[q])
            pieces[pl.ds(0, SIDE)] = got_f[k]
            pieces[pl.ds(SIDE, SIDE)] = got_d[q]

        cols = pl.ds(pl.multiple_of(c * CW, CW), CW)
        table = jnp.where(k >= first_direct, 0, SIDE)

        def blend(f, carry):
            nm = 0.5 * (pieces[f] + pieces[order[table + f]])
            if crossing:
                e = e_pieces[f, :, cols] + e_pieces[order[SIDE + f], :, cols]
            else:
                e = got_e[f, block, :, cols] + got_e[order[f], block, :, cols]
            blended[slot, 0, f] = nm
            blended[slot, 1, f] = 0.5 * e - 1.33 * nm
            return carry

        lax.fori_loop(0, SIDE, blend, 0)
        rows = pl.ds(pl.multiple_of(block * ROWS + seat * PIECE, PIECE), PIECE)

        def send(i, carry):
            to = seat_at(i)
            for n, out in enumerate((new_momentum, new_anchor)):
                remote(
                    blended.at[slot, n, to], out.at[rows, cols], b_send.at[slot, n], b_recv.at[k, n], {"farm": base + to}
                )
            return carry

        lax.fori_loop(1, SIDE, send, 0)
        for n, out in enumerate((new_momentum, new_anchor)):
            pltpu.make_async_copy(blended.at[slot, n, seat], out.at[rows, cols], own_sem.at[slot, n]).start()

    def make_early():
        for n in (0, 1):
            wait_bytes(state.at[n], load_s.at[n])

        def block_of(b, carry):
            rows = pl.ds(pl.multiple_of(b * ROWS, ROWS), ROWS)
            for c in range(col_blocks):
                e = state[0, c, rows] + 0.63 * state[1, c, rows]
                early[b, :, :, pl.ds(c * CW, CW)] = e.reshape(SIDE, PIECE, CW)
            return carry

        lax.fori_loop(0, row_blocks, block_of, 0)
        got_e[seat] = early[:, seat]

    e_peers = SIDE - 1 if crossing else FARMS - 1

    def send_early(first):
        def send(i, carry):
            to = seat_at(i)
            near = i < SIDE
            farm = jnp.where(near, base, across) + to
            remote(early.at[:, to], got_e.at[seat + jnp.where(near, 0, SIDE)], e_send, e_recv, {"farm": farm})
            return carry

        lax.fori_loop(first, jnp.minimum(first + plan.early_per, e_peers + 1), send, 0)

    def cross_early(b):
        @pl.when(b == 0)
        def _():
            wait_bytes(got_e.at[pl.ds(0, SIDE - 1)], e_recv)

        for q in range(crossing):
            e_to_cross[b, q] = got_e[order[2 * SIDE + q], b]
        remote(e_to_cross.at[b], got_ec.at[b], ec_send.at[b], ec_recv.at[b], mirror)

    e_steps = -(-e_peers // plan.early_per)

    def step(t, carry):
        def stage(lag, first, last, do):
            if first < last:
                pl.when((t >= first + lag) & (t < last + lag))(lambda: do(t - lag))

        def done(after, lag, catch_up, last):
            count = after + 1 - lag
            for at in catch_up:
                count = count + jnp.where(after >= at, 1, 0)
            return jnp.clip(count, 0, last)

        def stages(lag, catch_up, last, do):
            def one(k, carry):
                do(k)
                return carry

            lax.fori_loop(done(t - 1, lag, catch_up, last), done(t, lag, catch_up, last), one, 0)

        stage(0, 0, y_chunks, multiply)
        stage(0, y_chunks, chunks, wide_start)
        pl.when(t == 0)(load_rest)
        stage(1, 0, y_chunks, pass_on)
        stage(1, y_chunks, chunks, wide_pass_on)
        pl.when(t == 1)(make_early)
        pl.when((t >= 1) & (t < 1 + e_steps))(lambda: send_early((t - 1) * plan.early_per + 1))
        pl.when(t == 2)(make_order)
        stage(2, 0, y_chunks, finish_y)
        stages(plan.update_lag, plan.update_catch, y_chunks, lambda k: update(k, gradient_of))
        stage(WIDE_LAG, y_chunks, chunks, lambda k: update(k, wide_gradient_of))
        if crossing:
            stage(plan.early_cross, 0, row_blocks, cross_early)
            stages(plan.update_lag + 1, tuple(at + 1 for at in plan.update_catch), first_direct, cross)
        stages(plan.average_lag, plan.average_catch, chunks, average)
        if wide_chunks:

            def wides_done(after):
                return sum((jnp.where(after >= at, n, 0) for at, n in plan.wide_steps), jnp.int32(0))

            def one(m, carry):
                wide_part(m)
                return carry

            lax.fori_loop(wides_done(t - 1), wides_done(t), one, 0)

        return carry

    lax.fori_loop(0, chunks + 5, step, 0)

    for slot in range(SLOTS):
        wait_sent(slot)
        wait_blended(slot)
    wait_bytes(got_e.at[pl.ds(0, e_peers)], e_send)
    if wide_chunks:
        wait_bytes(wide_side, w_send)
    for q in range(wide_chunks):
        for i in range(6):
            wait_bytes(wide_y.at[q, i], wy_send.at[q, i])

    def last_across(q, carry):
        wait_bytes(got_d.at[q], d_send.at[q])
        return carry

    lax.fori_loop(0, plan.direct, last_across, 0)
    if crossing:

        def last_early(b, carry):
            wait_bytes(got_ec.at[b], ec_send.at[b])
            return carry

        def last_cross(k, carry):
            wait_bytes(got_c.at[k], c_send.at[k])
            return carry

        lax.fori_loop(0, row_blocks, last_early, 0)
        lax.fori_loop(0, first_direct, last_cross, 0)

    def last(k, carry):
        wait_bytes(got_f.at[k, pl.ds(0, SIDE - 1)], f_send.at[k])
        for n in range(2):
            wait_bytes(blended.at[0, n, pl.ds(0, SIDE - 1)], b_recv.at[k, n])
        return carry

    lax.fori_loop(0, chunks, last, 0)


def outer_step(plan, arrays):
    acts, weights = arrays[1], arrays[3]
    tokens = acts.shape[0]
    shard, width = weights.shape
    col_blocks, row_blocks = width // CW, shard // ROWS
    chunks = col_blocks * row_blocks
    crossing, wides = max(plan.crossing, 1), max(plan.wide_chunks, 1)
    f32 = jnp.float32
    dma = pltpu.SemaphoreType.DMA
    anywhere = pl.BlockSpec(memory_space=pl.ANY)
    wide = pltpu.VMEM((wides, YS, 2, ROWS, CW // 2), f32)
    return pl.pallas_call(
        functools.partial(kernel, plan),
        out_shape=[jax.ShapeDtypeStruct((shard, width), f32)] * 2,
        in_specs=[pl.BlockSpec(memory_space=pltpu.SMEM)] + [anywhere] * 7,
        out_specs=[anywhere] * 2,
        scratch_shapes=[
            pltpu.VMEM((row_blocks, 2 * YS, tokens, ROWS), jnp.bfloat16),
            pltpu.VMEM((col_blocks, tokens, CW), jnp.bfloat16),
            pltpu.VMEM((5, col_blocks, shard, CW), f32),
            pltpu.VMEM((SLOTS, 8, ROWS, CW), f32),
            pltpu.VMEM((chunks - plan.wide_chunks, 6, ROWS, CW), f32),
            pltpu.VMEM((chunks - plan.wide_chunks, ROWS, CW), f32),
            pltpu.VMEM((chunks, ROWS, CW), f32),
            pltpu.VMEM((chunks, SIDE, PIECE, CW), f32),
            pltpu.VMEM((chunks, crossing, PIECE, CW), f32),
            pltpu.VMEM((chunks, crossing, PIECE, CW), f32),
            pltpu.VMEM((FARMS, PIECE, CW), f32),
            pltpu.VMEM((SLOTS, 2, SIDE, PIECE, CW), f32),
            pltpu.VMEM((plan.direct, SIDE, PIECE, CW), f32),
            pltpu.VMEM((row_blocks, SIDE, PIECE, width), f32),
            pltpu.VMEM((SIDE if plan.crossing else FARMS, row_blocks, PIECE, width), f32),
            pltpu.VMEM((row_blocks, crossing, PIECE, width), f32),
            pltpu.VMEM((row_blocks, crossing, PIECE, width), f32),
            pltpu.VMEM((SIDE + crossing, PIECE, width), f32),
            wide,
            wide,
            wide,
            pltpu.VMEM((wides, 6, ROWS, CW // 2), f32),
            pltpu.SMEM((2 * SIDE + crossing,), jnp.int32),
            dma((row_blocks,)),
            dma((6,)),
            dma((SLOTS, 6)),
            dma((chunks, 6)),
            dma((SLOTS,)),
            dma((chunks,)),
            dma((chunks,)),
            dma((chunks,)),
            dma((chunks,)),
            dma((chunks,)),
            dma((plan.direct,)),
            dma((plan.direct,)),
            dma((SLOTS, 2)),
            dma((chunks, 2)),
            dma((SLOTS, 2)),
            dma,
            dma,
            dma((row_blocks,)),
            dma((row_blocks,)),
            dma,
            dma,
            dma((wides, 6)),
            dma((wides, 6)),
        ],
        compiler_params=pltpu.CompilerParams(
            collective_id=plan.number, has_side_effects=True, vmem_limit_bytes=60 << 20
        ),
        cost_estimate=pl.CostEstimate(
            flops=2 * tokens * 2 * YS * shard * width, bytes_accessed=24 << 20, transcendentals=shard * width
        ),
        name=f"outer_step_{plan.crossing}",
    )(*arrays)


def on_device(activations, out_grads, weights, anchor, adam_m, adam_v, momentum, partner):
    arrays = (partner, activations[0], out_grads[0], weights[0], anchor[0], adam_m[0], adam_v[0], momentum[0])
    c = jnp.sum((partner[:SIDE] >= SIDE).astype(jnp.int32))
    new_momentum, new_anchor = lax.switch((c > 4).astype(jnp.int32) + (c > 6).astype(jnp.int32), (functools.partial(outer_step, Plan(0, 4, 1, 3, ((1, 3), (2, 2), (3, 2), (4, 1), (5, 1), (7, 1), (9, 1), (11, 1)), 3, 4, 3, (), 5, ())), functools.partial(outer_step, Plan(1, 6, 1, 1, ((1, 2), (2, 2)), 3, 4, 3, (), 5, ())), functools.partial(outer_step, Plan(2, 8, 1, 0, (), 3, 4, 3, (), 5, ()))), arrays)
    return new_anchor[None], new_momentum[None]


def solution(mesh):
    split = P("farm", "fsdp", None)
    return jax.shard_map(
        on_device, mesh=mesh, in_specs=(split,) * 7 + (P(),), out_specs=(split, split), check_vma=False
    )
```

```python
import functools
from typing import NamedTuple

import jax
import jax.numpy as jnp
from jax import lax
from jax.experimental import pallas as pl
from jax.experimental.pallas import tpu as pltpu
from jax.sharding import PartitionSpec as P

MESH = pl.DeviceIdType.MESH
FARMS = 16
YS = 4
ROWS = 128
CW = 256
SLOTS = 4
SIDE = 8
PIECE = ROWS // SIDE
WIDE_LAG = 2


class Plan(NamedTuple):
    number: int
    crossing: int
    direct: int
    wide_chunks: int
    wide_steps: tuple
    early_per: int
    early_cross: int
    update_lag: int
    update_catch: tuple
    average_lag: int
    average_catch: tuple


def kernel(
    plan,
    partner, acts, grads, weights, anchor, adam_m, adam_v, momentum,
    new_momentum, new_anchor,
    acts_v, grads_v, state, part, got_y, got_x, mine, got_f, to_cross, got_c, pieces, blended,
    got_d, early, got_e, e_to_cross, got_ec, e_pieces, wide, wide_side, wide_sum, wide_y, order,
    load_a, load_s, y_send, y_recv, x_send, x_recv, f_send, f_recv, c_send, c_recv, d_send, d_recv, b_send, b_recv, own_sem,
    e_send, e_recv, ec_send, ec_recv, w_send, w_recv, wy_send, wy_recv,
):
    shard = weights.shape[0]
    width = weights.shape[1]
    tokens = acts.shape[0]
    col_blocks = width // CW
    row_blocks = shard // ROWS
    chunks = row_blocks * col_blocks
    crossing, wide_chunks = plan.crossing, plan.wide_chunks
    first_direct = chunks - plan.direct
    y_chunks = chunks - wide_chunks
    half_cw = CW // 2
    wide_block = y_chunks // col_blocks

    me = lax.axis_index("farm")
    place = lax.axis_index("fsdp")
    y, half = place // 2, lax.rem(place, 2)
    y_up, y_op, y_dn = lax.rem(y + 1, YS), lax.rem(y + 2, YS), lax.rem(y + 3, YS)
    up = {"fsdp": y_up * 2 + half}
    dn = {"fsdp": y_dn * 2 + half}
    side = {"fsdp": y * 2 + (1 - half)}
    base = me // SIDE * SIDE
    seat = me - base
    across = SIDE - base
    mirror = {"farm": across + seat}

    def seat_at(i):
        return lax.rem(seat + i, SIDE)

    barrier = pltpu.get_barrier_semaphore()
    for other in (up, dn, side):
        pl.semaphore_signal(barrier, inc=1, device_id=other, device_id_type=MESH)
    for i in range(1, SIDE):
        pl.semaphore_signal(barrier, inc=1, device_id={"farm": base + seat_at(i)}, device_id_type=MESH)
    for i in range(SIDE):
        pl.semaphore_signal(barrier, inc=1, device_id={"farm": across + seat_at(i)}, device_id_type=MESH)

    def load_acts(block):
        for s in range(2 * YS):
            pltpu.make_async_copy(
                acts.at[:, pl.ds(s * shard + block * ROWS, ROWS)], acts_v.at[block, s], load_a.at[block]
            ).start()

    def load_state(n, ref):
        for c in range(col_blocks):
            pltpu.make_async_copy(ref.at[:, pl.ds(c * CW, CW)], state.at[n, c], load_s.at[n]).start()

    def load_rest():
        load_state(0, anchor)
        load_state(1, momentum)
        for block in (*range(wide_block, row_blocks), *range(1, wide_block)):
            load_acts(block)
        load_state(2, weights)
        load_state(3, adam_m)
        load_state(4, adam_v)

    for c in range(col_blocks):
        pltpu.make_async_copy(grads.at[:, pl.ds(c * CW, CW)], grads_v.at[c], load_s.at[5]).start()
    load_acts(0)

    def wait_bytes(ref, sem):
        pltpu.make_async_copy(ref, ref, sem).wait()

    def remote(src, dst, send, recv, to):
        pltpu.make_async_remote_copy(
            src_ref=src, dst_ref=dst, send_sem=send, recv_sem=recv, device_id=to, device_id_type=MESH
        ).start()

    def product(block, s, cot):
        return lax.dot_general(acts_v[block, s], cot, (((0,), (0,)), ((), ())), preferred_element_type=jnp.float32)

    def wait_sent(slot):
        for j in range(6):
            wait_bytes(part.at[slot, 0], y_send.at[slot, j])
        wait_bytes(part.at[slot, 0], x_send.at[slot])

    wait_bytes(grads_v, load_s.at[5])

    def multiply(k):
        slot, block, c = lax.rem(k, SLOTS), k // col_blocks, lax.rem(k, col_blocks)

        @pl.when((c == 0) & (block < wide_block))
        def _():
            wait_bytes(acts_v.at[block], load_a.at[block])

        @pl.when(k >= SLOTS)
        def _():
            wait_sent(slot)

        def send(i, to):
            remote(part.at[slot, i], got_y.at[k, i], y_send.at[slot, i], y_recv.at[k, i], to)

        cot = grads_v[c]
        for i, (yd, h) in enumerate(((y_op, 0), (y_op, 1), (y_dn, 0), (y_up, 1), (y_up, 0), (y_dn, 1), (y, 0), (y, 1))):
            part[slot, i] = product(block, yd * 2 + h, cot)
            if i == 1:

                @pl.when(k == 0)
                def _():
                    pl.semaphore_wait(barrier, 3 + FARMS - 1)

                send(0, up)
                send(1, dn)
            if i == 2:
                send(2, dn)
            if i == 3:
                send(3, up)

    def pass_on(k):
        slot = lax.rem(k, SLOTS)
        for h, to in ((0, up), (1, dn)):
            wait_bytes(got_y.at[k, h], y_recv.at[k, h])
            i = 4 + h
            part[slot, i] += got_y[k, h]
            remote(part.at[slot, i], got_y.at[k, i], y_send.at[slot, i], y_recv.at[k, i], to)

    def finish_y(k):
        slot = lax.rem(k, SLOTS)
        for n, h in enumerate((1 - half, half)):
            wait_bytes(got_y.at[k, 2 + h], y_recv.at[k, 2 + h])
            wait_bytes(got_y.at[k, 4 + h], y_recv.at[k, 4 + h])
            part[slot, 6 + h] += got_y[k, 2 + h] + got_y[k, 4 + h]
            if n == 0:
                remote(part.at[slot, 6 + h], got_x.at[k], x_send.at[slot], x_recv.at[k], side)

    def gradient_of(k):
        wait_bytes(got_x.at[k], x_recv.at[k])
        return part[lax.rem(k, SLOTS), 6 + half] + got_x[k]

    def wide_part(m):
        q, d = m // YS, lax.rem(m, YS)
        k = y_chunks + q
        block, c = k // col_blocks, lax.rem(k, col_blocks)

        @pl.when(m == 0)
        def _():
            for b in range(wide_block, row_blocks):
                wait_bytes(acts_v.at[b], load_a.at[b])

        cot = grads_v[c]
        yd = lax.rem(y + d, YS)
        for h, to in ((1 - half, wide_side), (half, wide)):
            term = product(block, yd * 2 + h, cot)
            for n in range(2):
                to[q, d, n] = term[:, n * half_cw : (n + 1) * half_cw]
        remote(wide_side.at[q, d], wide_sum.at[q, d], w_send, w_recv, side)

    def wide_start(k):
        q = k - y_chunks

        @pl.when(q == 0)
        def _():
            wait_bytes(wide_sum, w_recv)

        def send(i, d, n, to):
            remote(wide.at[q, d, n], wide_y.at[q, i], wy_send.at[q, i], wy_recv.at[q, i], to)

        wide[q, 2] += wide_sum[q, 2]
        send(0, 2, 0, up)
        send(1, 2, 1, dn)
        wide[q, 1] += wide_sum[q, 1]
        wide[q, 3] += wide_sum[q, 3]
        send(2, 3, 0, dn)
        send(3, 1, 1, up)
        wide[q, 0] += wide_sum[q, 0]

    def wide_pass_on(k):
        q = k - y_chunks
        for n, to, d in ((0, up, 1), (1, dn, 3)):
            wait_bytes(wide_y.at[q, n], wy_recv.at[q, n])
            i = 4 + n
            wide[q, d, n] += wide_y[q, n]
            remote(wide.at[q, d, n], wide_y.at[q, i], wy_send.at[q, i], wy_recv.at[q, i], to)

    def wide_gradient_of(k):
        q = k - y_chunks
        halves = []
        for n in range(2):
            for i in (2 + n, 4 + n):
                wait_bytes(wide_y.at[q, i], wy_recv.at[q, i])
            halves.append(wide[q, 0, n] + wide_y[q, 2 + n] + wide_y[q, 4 + n])
        return jnp.concatenate(halves, axis=1)

    def update(k, gradient_sum):
        block, c = k // col_blocks, lax.rem(k, col_blocks)

        @pl.when(k == 0)
        def _():
            for n in (2, 3, 4):
                wait_bytes(state.at[n], load_s.at[n])

        rows = pl.ds(pl.multiple_of(block * ROWS, ROWS), ROWS)
        gradient = gradient_sum(k) * (1.0 / (tokens * 2 * YS))
        anchor_c, mom_c, w_c = state[0, c, rows], state[1, c, rows], state[2, c, rows]
        m1 = 0.9 * state[3, c, rows] + 0.1 * gradient
        v1 = 0.95 * state[4, c, rows] + 0.05 * gradient * gradient
        inner = w_c - 0.3 * (m1 / (jnp.sqrt(v1) + 1e-08) + 0.1 * w_c)
        mine[k] = 0.9 * mom_c + (anchor_c - inner)
        got_f[k, seat] = mine[k, pl.ds(pl.multiple_of(seat * PIECE, PIECE), PIECE)]

        def piece(to):
            return mine.at[k, pl.ds(pl.multiple_of(to * PIECE, PIECE), PIECE)]

        @pl.when(k >= first_direct)
        def _():
            def send_across(i, carry):
                to, q = seat_at(i), k - first_direct
                remote(piece(to), got_d.at[q, seat], d_send.at[q], d_recv.at[q], {"farm": across + to})
                return carry

            lax.fori_loop(0, SIDE, send_across, 0)

        def send(i, carry):
            to = seat_at(i)
            remote(piece(to), got_f.at[k, seat], f_send.at[k], f_recv.at[k], {"farm": base + to})
            return carry

        lax.fori_loop(1, SIDE, send, 0)

    def make_order():
        crosses = [
            [((partner[h * SIDE + g] >= SIDE) != (h == 1)).astype(jnp.int32) for g in range(SIDE)] for h in range(2)
        ]
        ranks = []
        for flags in crosses:
            total, rank = jnp.int32(0), []
            for flag in flags:
                rank.append(total)
                total = total + flag
            ranks.append(rank)
        low = base == 0
        flags = [jnp.where(low, a, b) for a, b in zip(*crosses)]
        rank = [jnp.where(low, a, b) for a, b in zip(*ranks)]
        rank_there = [jnp.where(low, b, a) for a, b in zip(*ranks)]
        for f in range(SIDE):
            p = partner[base + f]
            seat_p = jnp.where(p >= SIDE, p - SIDE, p)
            order[f] = jnp.where(flags[f] == 1, SIDE, 0) + seat_p
            there = jnp.int32(0)
            for g in range(SIDE):
                there = there + jnp.where(seat_p == g, rank_there[g], 0)
            order[SIDE + f] = jnp.where(flags[f] == 1, SIDE + there, seat_p)
        for q in range(crossing):
            farm = jnp.int32(0)
            for g in range(SIDE):
                farm = farm + jnp.where(rank[g] == q, flags[g] * g, 0)
            order[2 * SIDE + q] = farm

    def cross(k):
        wait_bytes(got_f.at[k, pl.ds(0, SIDE - 1)], f_recv.at[k])
        pieces[pl.ds(0, SIDE)] = got_f[k]
        for q in range(crossing):
            to_cross[k, q] = pieces[order[2 * SIDE + q]]
        remote(to_cross.at[k], got_c.at[k], c_send.at[k], c_recv.at[k], mirror)

    def wait_blended(slot):
        for n in range(2):
            wait_bytes(blended.at[slot, n, pl.ds(0, SIDE - 1)], b_send.at[slot, n])
            wait_bytes(blended.at[slot, n, 0], own_sem.at[slot, n])

    def average(k):
        slot, block, c = lax.rem(k, SLOTS), k // col_blocks, lax.rem(k, col_blocks)

        if crossing:

            @pl.when(c == 0)
            def _():
                wait_bytes(got_ec.at[block], ec_recv.at[block])
                e_pieces[pl.ds(0, SIDE)] = got_e[:, block]
                e_pieces[pl.ds(SIDE, crossing)] = got_ec[block]

        else:

            @pl.when(k == 0)
            def _():
                wait_bytes(got_e.at[pl.ds(0, FARMS - 1)], e_recv)

        @pl.when(k >= SLOTS)
        def _():
            wait_blended(slot)

        if crossing:

            @pl.when(k < first_direct)
            def _():
                wait_bytes(got_c.at[k], c_recv.at[k])
                pieces[pl.ds(0, SIDE)] = got_f[k]
                pieces[pl.ds(SIDE, crossing)] = got_c[k]

        @pl.when(k >= first_direct)
        def _():
            q = k - first_direct
            wait_bytes(got_f.at[k, pl.ds(0, SIDE - 1)], f_recv.at[k])
            wait_bytes(got_d.at[q], d_recv.at[q])
            pieces[pl.ds(0, SIDE)] = got_f[k]
            pieces[pl.ds(SIDE, SIDE)] = got_d[q]

        cols = pl.ds(pl.multiple_of(c * CW, CW), CW)
        table = jnp.where(k >= first_direct, 0, SIDE)

        def blend(f, carry):
            nm = 0.5 * (pieces[f] + pieces[order[table + f]])
            if crossing:
                e = e_pieces[f, :, cols] + e_pieces[order[SIDE + f], :, cols]
            else:
                e = got_e[f, block, :, cols] + got_e[order[f], block, :, cols]
            blended[slot, 0, f] = nm
            blended[slot, 1, f] = 0.5 * e - 1.33 * nm
            return carry

        lax.fori_loop(0, SIDE, blend, 0)
        rows = pl.ds(pl.multiple_of(block * ROWS + seat * PIECE, PIECE), PIECE)

        def send(i, carry):
            to = seat_at(i)
            for n, out in enumerate((new_momentum, new_anchor)):
                remote(
                    blended.at[slot, n, to], out.at[rows, cols], b_send.at[slot, n], b_recv.at[k, n], {"farm": base + to}
                )
            return carry

        lax.fori_loop(1, SIDE, send, 0)
        for n, out in enumerate((new_momentum, new_anchor)):
            pltpu.make_async_copy(blended.at[slot, n, seat], out.at[rows, cols], own_sem.at[slot, n]).start()

    def make_early():
        for n in (0, 1):
            wait_bytes(state.at[n], load_s.at[n])

        def block_of(b, carry):
            rows = pl.ds(pl.multiple_of(b * ROWS, ROWS), ROWS)
            for c in range(col_blocks):
                e = state[0, c, rows] + 0.63 * state[1, c, rows]
                early[b, :, :, pl.ds(c * CW, CW)] = e.reshape(SIDE, PIECE, CW)
            return carry

        lax.fori_loop(0, row_blocks, block_of, 0)
        got_e[seat] = early[:, seat]

    e_peers = SIDE - 1 if crossing else FARMS - 1

    def send_early(first):
        def send(i, carry):
            to = seat_at(i)
            near = i < SIDE
            farm = jnp.where(near, base, across) + to
            remote(early.at[:, to], got_e.at[seat + jnp.where(near, 0, SIDE)], e_send, e_recv, {"farm": farm})
            return carry

        lax.fori_loop(first, jnp.minimum(first + plan.early_per, e_peers + 1), send, 0)

    def cross_early(b):
        @pl.when(b == 0)
        def _():
            wait_bytes(got_e.at[pl.ds(0, SIDE - 1)], e_recv)

        for q in range(crossing):
            e_to_cross[b, q] = got_e[order[2 * SIDE + q], b]
        remote(e_to_cross.at[b], got_ec.at[b], ec_send.at[b], ec_recv.at[b], mirror)

    e_steps = -(-e_peers // plan.early_per)

    def step(t, carry):
        def stage(lag, first, last, do):
            if first < last:
                pl.when((t >= first + lag) & (t < last + lag))(lambda: do(t - lag))

        def done(after, lag, catch_up, last):
            count = after + 1 - lag
            for at in catch_up:
                count = count + jnp.where(after >= at, 1, 0)
            return jnp.clip(count, 0, last)

        def stages(lag, catch_up, last, do):
            def one(k, carry):
                do(k)
                return carry

            lax.fori_loop(done(t - 1, lag, catch_up, last), done(t, lag, catch_up, last), one, 0)

        stage(0, 0, y_chunks, multiply)
        stage(0, y_chunks, chunks, wide_start)
        pl.when(t == 0)(load_rest)
        stage(1, 0, y_chunks, pass_on)
        stage(1, y_chunks, chunks, wide_pass_on)
        pl.when(t == 1)(make_early)
        pl.when((t >= 1) & (t < 1 + e_steps))(lambda: send_early((t - 1) * plan.early_per + 1))
        pl.when(t == 2)(make_order)
        stage(2, 0, y_chunks, finish_y)
        stages(plan.update_lag, plan.update_catch, y_chunks, lambda k: update(k, gradient_of))
        stage(WIDE_LAG, y_chunks, chunks, lambda k: update(k, wide_gradient_of))
        if crossing:
            stage(plan.early_cross, 0, row_blocks, cross_early)
            stages(plan.update_lag + 1, tuple(at + 1 for at in plan.update_catch), first_direct, cross)
        stages(plan.average_lag, plan.average_catch, chunks, average)
        if wide_chunks:

            def wides_done(after):
                return sum((jnp.where(after >= at, n, 0) for at, n in plan.wide_steps), jnp.int32(0))

            def one(m, carry):
                wide_part(m)
                return carry

            lax.fori_loop(wides_done(t - 1), wides_done(t), one, 0)

        return carry

    lax.fori_loop(0, chunks + 5, step, 0)

    for slot in range(SLOTS):
        wait_sent(slot)
        wait_blended(slot)
    wait_bytes(got_e.at[pl.ds(0, e_peers)], e_send)
    if wide_chunks:
        wait_bytes(wide_side, w_send)
    for q in range(wide_chunks):
        for i in range(6):
            wait_bytes(wide_y.at[q, i], wy_send.at[q, i])

    def last_across(q, carry):
        wait_bytes(got_d.at[q], d_send.at[q])
        return carry

    lax.fori_loop(0, plan.direct, last_across, 0)
    if crossing:

        def last_early(b, carry):
            wait_bytes(got_ec.at[b], ec_send.at[b])
            return carry

        def last_cross(k, carry):
            wait_bytes(got_c.at[k], c_send.at[k])
            return carry

        lax.fori_loop(0, row_blocks, last_early, 0)
        lax.fori_loop(0, first_direct, last_cross, 0)

    def last(k, carry):
        wait_bytes(got_f.at[k, pl.ds(0, SIDE - 1)], f_send.at[k])
        for n in range(2):
            wait_bytes(blended.at[0, n, pl.ds(0, SIDE - 1)], b_recv.at[k, n])
        return carry

    lax.fori_loop(0, chunks, last, 0)


def outer_step(plan, arrays):
    acts, weights = arrays[1], arrays[3]
    tokens = acts.shape[0]
    shard, width = weights.shape
    col_blocks, row_blocks = width // CW, shard // ROWS
    chunks = col_blocks * row_blocks
    crossing, wides = max(plan.crossing, 1), max(plan.wide_chunks, 1)
    f32 = jnp.float32
    dma = pltpu.SemaphoreType.DMA
    anywhere = pl.BlockSpec(memory_space=pl.ANY)
    wide = pltpu.VMEM((wides, YS, 2, ROWS, CW // 2), f32)
    return pl.pallas_call(
        functools.partial(kernel, plan),
        out_shape=[jax.ShapeDtypeStruct((shard, width), f32)] * 2,
        in_specs=[pl.BlockSpec(memory_space=pltpu.SMEM)] + [anywhere] * 7,
        out_specs=[anywhere] * 2,
        scratch_shapes=[
            pltpu.VMEM((row_blocks, 2 * YS, tokens, ROWS), jnp.bfloat16),
            pltpu.VMEM((col_blocks, tokens, CW), jnp.bfloat16),
            pltpu.VMEM((5, col_blocks, shard, CW), f32),
            pltpu.VMEM((SLOTS, 8, ROWS, CW), f32),
            pltpu.VMEM((chunks - plan.wide_chunks, 6, ROWS, CW), f32),
            pltpu.VMEM((chunks - plan.wide_chunks, ROWS, CW), f32),
            pltpu.VMEM((chunks, ROWS, CW), f32),
            pltpu.VMEM((chunks, SIDE, PIECE, CW), f32),
            pltpu.VMEM((chunks, crossing, PIECE, CW), f32),
            pltpu.VMEM((chunks, crossing, PIECE, CW), f32),
            pltpu.VMEM((FARMS, PIECE, CW), f32),
            pltpu.VMEM((SLOTS, 2, SIDE, PIECE, CW), f32),
            pltpu.VMEM((plan.direct, SIDE, PIECE, CW), f32),
            pltpu.VMEM((row_blocks, SIDE, PIECE, width), f32),
            pltpu.VMEM((SIDE if plan.crossing else FARMS, row_blocks, PIECE, width), f32),
            pltpu.VMEM((row_blocks, crossing, PIECE, width), f32),
            pltpu.VMEM((row_blocks, crossing, PIECE, width), f32),
            pltpu.VMEM((SIDE + crossing, PIECE, width), f32),
            wide,
            wide,
            wide,
            pltpu.VMEM((wides, 6, ROWS, CW // 2), f32),
            pltpu.SMEM((2 * SIDE + crossing,), jnp.int32),
            dma((row_blocks,)),
            dma((6,)),
            dma((SLOTS, 6)),
            dma((chunks, 6)),
            dma((SLOTS,)),
            dma((chunks,)),
            dma((chunks,)),
            dma((chunks,)),
            dma((chunks,)),
            dma((chunks,)),
            dma((plan.direct,)),
            dma((plan.direct,)),
            dma((SLOTS, 2)),
            dma((chunks, 2)),
            dma((SLOTS, 2)),
            dma,
            dma,
            dma((row_blocks,)),
            dma((row_blocks,)),
            dma,
            dma,
            dma((wides, 6)),
            dma((wides, 6)),
        ],
        compiler_params=pltpu.CompilerParams(
            collective_id=plan.number, has_side_effects=True, vmem_limit_bytes=60 << 20
        ),
        cost_estimate=pl.CostEstimate(
            flops=2 * tokens * 2 * YS * shard * width, bytes_accessed=24 << 20, transcendentals=shard * width
        ),
        name=f"outer_step_{plan.crossing}",
    )(*arrays)


def on_device(activations, out_grads, weights, anchor, adam_m, adam_v, momentum, partner):
    arrays = (partner, activations[0], out_grads[0], weights[0], anchor[0], adam_m[0], adam_v[0], momentum[0])
    c = jnp.sum((partner[:SIDE] >= SIDE).astype(jnp.int32))
    new_momentum, new_anchor = lax.switch((c > 4).astype(jnp.int32) + (c > 6).astype(jnp.int32), (functools.partial(outer_step, Plan(0, 4, 1, 3, ((1, 3), (2, 2), (3, 2), (4, 1), (5, 1), (7, 1), (9, 1), (11, 1)), 3, 4, 3, (), 5, ())), functools.partial(outer_step, Plan(1, 6, 1, 2, ((1, 3), (2, 2), (3, 2), (4, 1)), 3, 4, 3, (), 5, ())), functools.partial(outer_step, Plan(2, 8, 1, 0, (), 3, 4, 3, (), 5, ()))), arrays)
    return new_anchor[None], new_momentum[None]


def solution(mesh):
    split = P("farm", "fsdp", None)
    return jax.shard_map(
        on_device, mesh=mesh, in_specs=(split,) * 7 + (P(),), out_specs=(split, split), check_vma=False
    )
```

```python
import functools
from typing import NamedTuple

import jax
import jax.numpy as jnp
from jax import lax
from jax.experimental import pallas as pl
from jax.experimental.pallas import tpu as pltpu
from jax.sharding import PartitionSpec as P

MESH = pl.DeviceIdType.MESH
FARMS = 16
YS = 4
ROWS = 128
CW = 256
SLOTS = 4
SIDE = 8
PIECE = ROWS // SIDE
WIDE_LAG = 2


class Plan(NamedTuple):
    number: int
    crossing: int
    direct: int
    wide_chunks: int
    wide_steps: tuple
    early_per: int
    early_cross: int
    update_lag: int
    update_catch: tuple
    average_lag: int
    average_catch: tuple


def kernel(
    plan,
    partner, acts, grads, weights, anchor, adam_m, adam_v, momentum,
    new_momentum, new_anchor,
    acts_v, grads_v, state, part, got_y, got_x, mine, got_f, to_cross, got_c, pieces, blended,
    got_d, early, got_e, e_to_cross, got_ec, e_pieces, wide, wide_side, wide_sum, wide_y, order,
    load_a, load_s, y_send, y_recv, x_send, x_recv, f_send, f_recv, c_send, c_recv, d_send, d_recv, b_send, b_recv, own_sem,
    e_send, e_recv, ec_send, ec_recv, w_send, w_recv, wy_send, wy_recv,
):
    shard = weights.shape[0]
    width = weights.shape[1]
    tokens = acts.shape[0]
    col_blocks = width // CW
    row_blocks = shard // ROWS
    chunks = row_blocks * col_blocks
    crossing, wide_chunks = plan.crossing, plan.wide_chunks
    first_direct = chunks - plan.direct
    y_chunks = chunks - wide_chunks
    half_cw = CW // 2
    wide_block = y_chunks // col_blocks

    me = lax.axis_index("farm")
    place = lax.axis_index("fsdp")
    y, half = place // 2, lax.rem(place, 2)
    y_up, y_op, y_dn = lax.rem(y + 1, YS), lax.rem(y + 2, YS), lax.rem(y + 3, YS)
    up = {"fsdp": y_up * 2 + half}
    dn = {"fsdp": y_dn * 2 + half}
    side = {"fsdp": y * 2 + (1 - half)}
    base = me // SIDE * SIDE
    seat = me - base
    across = SIDE - base
    mirror = {"farm": across + seat}

    def seat_at(i):
        return lax.rem(seat + i, SIDE)

    def load_acts(block):
        for s in range(2 * YS):
            pltpu.make_async_copy(
                acts.at[:, pl.ds(s * shard + block * ROWS, ROWS)], acts_v.at[block, s], load_a.at[block]
            ).start()

    def load_state(n, ref):
        for c in range(col_blocks):
            pltpu.make_async_copy(ref.at[:, pl.ds(c * CW, CW)], state.at[n, c], load_s.at[n]).start()

    def load_rest():
        load_state(0, anchor)
        load_state(1, momentum)
        for block in (*range(wide_block, row_blocks), *range(1, wide_block)):
            load_acts(block)
        load_state(2, weights)
        load_state(3, adam_m)
        load_state(4, adam_v)

    for c in range(col_blocks):
        pltpu.make_async_copy(grads.at[:, pl.ds(c * CW, CW)], grads_v.at[c], load_s.at[5]).start()
    load_acts(0)

    barrier = pltpu.get_barrier_semaphore()
    for other in (up, dn, side):
        pl.semaphore_signal(barrier, inc=1, device_id=other, device_id_type=MESH)
    for i in range(1, SIDE):
        pl.semaphore_signal(barrier, inc=1, device_id={"farm": base + seat_at(i)}, device_id_type=MESH)
    for i in range(SIDE):
        pl.semaphore_signal(barrier, inc=1, device_id={"farm": across + seat_at(i)}, device_id_type=MESH)

    def wait_bytes(ref, sem):
        pltpu.make_async_copy(ref, ref, sem).wait()

    def remote(src, dst, send, recv, to):
        pltpu.make_async_remote_copy(
            src_ref=src, dst_ref=dst, send_sem=send, recv_sem=recv, device_id=to, device_id_type=MESH
        ).start()

    def product(block, s, cot):
        return lax.dot_general(acts_v[block, s], cot, (((0,), (0,)), ((), ())), preferred_element_type=jnp.float32)

    def wait_sent(slot):
        for j in range(6):
            wait_bytes(part.at[slot, 0], y_send.at[slot, j])
        wait_bytes(part.at[slot, 0], x_send.at[slot])

    wait_bytes(grads_v, load_s.at[5])

    def multiply(k):
        slot, block, c = lax.rem(k, SLOTS), k // col_blocks, lax.rem(k, col_blocks)

        @pl.when((c == 0) & (block < wide_block))
        def _():
            wait_bytes(acts_v.at[block], load_a.at[block])

        @pl.when(k >= SLOTS)
        def _():
            wait_sent(slot)

        def send(i, to):
            remote(part.at[slot, i], got_y.at[k, i], y_send.at[slot, i], y_recv.at[k, i], to)

        cot = grads_v[c]
        for i, (yd, h) in enumerate(((y_op, 0), (y_op, 1), (y_dn, 0), (y_up, 1), (y_up, 0), (y_dn, 1), (y, 0), (y, 1))):
            part[slot, i] = product(block, yd * 2 + h, cot)
            if i == 1:

                @pl.when(k == 0)
                def _():
                    pl.semaphore_wait(barrier, 3 + FARMS - 1)

                send(0, up)
                send(1, dn)
            if i == 2:
                send(2, dn)
            if i == 3:
                send(3, up)

    def pass_on(k):
        slot = lax.rem(k, SLOTS)
        for h, to in ((0, up), (1, dn)):
            wait_bytes(got_y.at[k, h], y_recv.at[k, h])
            i = 4 + h
            part[slot, i] += got_y[k, h]
            remote(part.at[slot, i], got_y.at[k, i], y_send.at[slot, i], y_recv.at[k, i], to)

    def finish_y(k):
        slot = lax.rem(k, SLOTS)
        for n, h in enumerate((1 - half, half)):
            wait_bytes(got_y.at[k, 2 + h], y_recv.at[k, 2 + h])
            wait_bytes(got_y.at[k, 4 + h], y_recv.at[k, 4 + h])
            part[slot, 6 + h] += got_y[k, 2 + h] + got_y[k, 4 + h]
            if n == 0:
                remote(part.at[slot, 6 + h], got_x.at[k], x_send.at[slot], x_recv.at[k], side)

    def gradient_of(k):
        wait_bytes(got_x.at[k], x_recv.at[k])
        return part[lax.rem(k, SLOTS), 6 + half] + got_x[k]

    def wide_part(m):
        q, d = m // YS, lax.rem(m, YS)
        k = y_chunks + q
        block, c = k // col_blocks, lax.rem(k, col_blocks)

        @pl.when(m == 0)
        def _():
            for b in range(wide_block, row_blocks):
                wait_bytes(acts_v.at[b], load_a.at[b])

        cot = grads_v[c]
        yd = lax.rem(y + d, YS)
        for h, to in ((1 - half, wide_side), (half, wide)):
            term = product(block, yd * 2 + h, cot)
            for n in range(2):
                to[q, d, n] = term[:, n * half_cw : (n + 1) * half_cw]
        remote(wide_side.at[q, d], wide_sum.at[q, d], w_send, w_recv, side)

    def wide_start(k):
        q = k - y_chunks

        @pl.when(q == 0)
        def _():
            wait_bytes(wide_sum, w_recv)

        def send(i, d, n, to):
            remote(wide.at[q, d, n], wide_y.at[q, i], wy_send.at[q, i], wy_recv.at[q, i], to)

        wide[q, 2] += wide_sum[q, 2]
        send(0, 2, 0, up)
        send(1, 2, 1, dn)
        wide[q, 1] += wide_sum[q, 1]
        wide[q, 3] += wide_sum[q, 3]
        send(2, 3, 0, dn)
        send(3, 1, 1, up)
        wide[q, 0] += wide_sum[q, 0]

    def wide_pass_on(k):
        q = k - y_chunks
        for n, to, d in ((0, up, 1), (1, dn, 3)):
            wait_bytes(wide_y.at[q, n], wy_recv.at[q, n])
            i = 4 + n
            wide[q, d, n] += wide_y[q, n]
            remote(wide.at[q, d, n], wide_y.at[q, i], wy_send.at[q, i], wy_recv.at[q, i], to)

    def wide_gradient_of(k):
        q = k - y_chunks
        halves = []
        for n in range(2):
            for i in (2 + n, 4 + n):
                wait_bytes(wide_y.at[q, i], wy_recv.at[q, i])
            halves.append(wide[q, 0, n] + wide_y[q, 2 + n] + wide_y[q, 4 + n])
        return jnp.concatenate(halves, axis=1)

    def update(k, gradient_sum):
        block, c = k // col_blocks, lax.rem(k, col_blocks)

        @pl.when(k == 0)
        def _():
            for n in (2, 3, 4):
                wait_bytes(state.at[n], load_s.at[n])

        rows = pl.ds(pl.multiple_of(block * ROWS, ROWS), ROWS)
        gradient = gradient_sum(k) * (1.0 / (tokens * 2 * YS))
        anchor_c, mom_c, w_c = state[0, c, rows], state[1, c, rows], state[2, c, rows]
        m1 = 0.9 * state[3, c, rows] + 0.1 * gradient
        v1 = 0.95 * state[4, c, rows] + 0.05 * gradient * gradient
        inner = w_c - 0.3 * (m1 / (jnp.sqrt(v1) + 1e-08) + 0.1 * w_c)
        mine[k] = 0.9 * mom_c + (anchor_c - inner)
        got_f[k, seat] = mine[k, pl.ds(pl.multiple_of(seat * PIECE, PIECE), PIECE)]

        def piece(to):
            return mine.at[k, pl.ds(pl.multiple_of(to * PIECE, PIECE), PIECE)]

        @pl.when(k >= first_direct)
        def _():
            def send_across(i, carry):
                to, q = seat_at(i), k - first_direct
                remote(piece(to), got_d.at[q, seat], d_send.at[q], d_recv.at[q], {"farm": across + to})
                return carry

            lax.fori_loop(0, SIDE, send_across, 0)

        def send(i, carry):
            to = seat_at(i)
            remote(piece(to), got_f.at[k, seat], f_send.at[k], f_recv.at[k], {"farm": base + to})
            return carry

        lax.fori_loop(1, SIDE, send, 0)

    def make_order():
        crosses = [
            [((partner[h * SIDE + g] >= SIDE) != (h == 1)).astype(jnp.int32) for g in range(SIDE)] for h in range(2)
        ]
        ranks = []
        for flags in crosses:
            total, rank = jnp.int32(0), []
            for flag in flags:
                rank.append(total)
                total = total + flag
            ranks.append(rank)
        low = base == 0
        flags = [jnp.where(low, a, b) for a, b in zip(*crosses)]
        rank = [jnp.where(low, a, b) for a, b in zip(*ranks)]
        rank_there = [jnp.where(low, b, a) for a, b in zip(*ranks)]
        for f in range(SIDE):
            p = partner[base + f]
            seat_p = jnp.where(p >= SIDE, p - SIDE, p)
            order[f] = jnp.where(flags[f] == 1, SIDE, 0) + seat_p
            there = jnp.int32(0)
            for g in range(SIDE):
                there = there + jnp.where(seat_p == g, rank_there[g], 0)
            order[SIDE + f] = jnp.where(flags[f] == 1, SIDE + there, seat_p)
        for q in range(crossing):
            farm = jnp.int32(0)
            for g in range(SIDE):
                farm = farm + jnp.where(rank[g] == q, flags[g] * g, 0)
            order[2 * SIDE + q] = farm

    def cross(k):
        wait_bytes(got_f.at[k, pl.ds(0, SIDE - 1)], f_recv.at[k])
        pieces[pl.ds(0, SIDE)] = got_f[k]
        for q in range(crossing):
            to_cross[k, q] = pieces[order[2 * SIDE + q]]
        remote(to_cross.at[k], got_c.at[k], c_send.at[k], c_recv.at[k], mirror)

    def wait_blended(slot):
        for n in range(2):
            wait_bytes(blended.at[slot, n, pl.ds(0, SIDE - 1)], b_send.at[slot, n])
            wait_bytes(blended.at[slot, n, 0], own_sem.at[slot, n])

    def average(k):
        slot, block, c = lax.rem(k, SLOTS), k // col_blocks, lax.rem(k, col_blocks)

        if crossing:

            @pl.when(c == 0)
            def _():
                wait_bytes(got_ec.at[block], ec_recv.at[block])
                e_pieces[pl.ds(0, SIDE)] = got_e[:, block]
                e_pieces[pl.ds(SIDE, crossing)] = got_ec[block]

        else:

            @pl.when(k == 0)
            def _():
                wait_bytes(got_e.at[pl.ds(0, FARMS - 1)], e_recv)

        @pl.when(k >= SLOTS)
        def _():
            wait_blended(slot)

        if crossing:

            @pl.when(k < first_direct)
            def _():
                wait_bytes(got_c.at[k], c_recv.at[k])
                pieces[pl.ds(0, SIDE)] = got_f[k]
                pieces[pl.ds(SIDE, crossing)] = got_c[k]

        @pl.when(k >= first_direct)
        def _():
            q = k - first_direct
            wait_bytes(got_f.at[k, pl.ds(0, SIDE - 1)], f_recv.at[k])
            wait_bytes(got_d.at[q], d_recv.at[q])
            pieces[pl.ds(0, SIDE)] = got_f[k]
            pieces[pl.ds(SIDE, SIDE)] = got_d[q]

        cols = pl.ds(pl.multiple_of(c * CW, CW), CW)
        table = jnp.where(k >= first_direct, 0, SIDE)

        def blend(f, carry):
            nm = 0.5 * (pieces[f] + pieces[order[table + f]])
            if crossing:
                e = e_pieces[f, :, cols] + e_pieces[order[SIDE + f], :, cols]
            else:
                e = got_e[f, block, :, cols] + got_e[order[f], block, :, cols]
            blended[slot, 0, f] = nm
            blended[slot, 1, f] = 0.5 * e - 1.33 * nm
            return carry

        lax.fori_loop(0, SIDE, blend, 0)
        rows = pl.ds(pl.multiple_of(block * ROWS + seat * PIECE, PIECE), PIECE)

        def send(i, carry):
            to = seat_at(i)
            for n, out in enumerate((new_momentum, new_anchor)):
                remote(
                    blended.at[slot, n, to], out.at[rows, cols], b_send.at[slot, n], b_recv.at[k, n], {"farm": base + to}
                )
            return carry

        lax.fori_loop(1, SIDE, send, 0)
        for n, out in enumerate((new_momentum, new_anchor)):
            pltpu.make_async_copy(blended.at[slot, n, seat], out.at[rows, cols], own_sem.at[slot, n]).start()

    def make_early():
        for n in (0, 1):
            wait_bytes(state.at[n], load_s.at[n])

        def block_of(b, carry):
            rows = pl.ds(pl.multiple_of(b * ROWS, ROWS), ROWS)
            for c in range(col_blocks):
                e = state[0, c, rows] + 0.63 * state[1, c, rows]
                early[b, :, :, pl.ds(c * CW, CW)] = e.reshape(SIDE, PIECE, CW)
            return carry

        lax.fori_loop(0, row_blocks, block_of, 0)
        got_e[seat] = early[:, seat]

    e_peers = SIDE - 1 if crossing else FARMS - 1

    def send_early(first):
        def send(i, carry):
            to = seat_at(i)
            near = i < SIDE
            farm = jnp.where(near, base, across) + to
            remote(early.at[:, to], got_e.at[seat + jnp.where(near, 0, SIDE)], e_send, e_recv, {"farm": farm})
            return carry

        lax.fori_loop(first, jnp.minimum(first + plan.early_per, e_peers + 1), send, 0)

    def cross_early(b):
        @pl.when(b == 0)
        def _():
            wait_bytes(got_e.at[pl.ds(0, SIDE - 1)], e_recv)

        for q in range(crossing):
            e_to_cross[b, q] = got_e[order[2 * SIDE + q], b]
        remote(e_to_cross.at[b], got_ec.at[b], ec_send.at[b], ec_recv.at[b], mirror)

    e_steps = -(-e_peers // plan.early_per)

    def step(t, carry):
        def stage(lag, first, last, do):
            if first < last:
                pl.when((t >= first + lag) & (t < last + lag))(lambda: do(t - lag))

        def done(after, lag, catch_up, last):
            count = after + 1 - lag
            for at in catch_up:
                count = count + jnp.where(after >= at, 1, 0)
            return jnp.clip(count, 0, last)

        def stages(lag, catch_up, last, do):
            def one(k, carry):
                do(k)
                return carry

            lax.fori_loop(done(t - 1, lag, catch_up, last), done(t, lag, catch_up, last), one, 0)

        stage(0, 0, y_chunks, multiply)
        stage(0, y_chunks, chunks, wide_start)
        pl.when(t == 0)(load_rest)
        stage(1, 0, y_chunks, pass_on)
        stage(1, y_chunks, chunks, wide_pass_on)
        pl.when(t == 1)(make_early)
        pl.when((t >= 1) & (t < 1 + e_steps))(lambda: send_early((t - 1) * plan.early_per + 1))
        pl.when(t == 2)(make_order)
        stage(2, 0, y_chunks, finish_y)
        stages(plan.update_lag, plan.update_catch, y_chunks, lambda k: update(k, gradient_of))
        stage(WIDE_LAG, y_chunks, chunks, lambda k: update(k, wide_gradient_of))
        if crossing:
            stage(plan.early_cross, 0, row_blocks, cross_early)
            stages(plan.update_lag + 1, tuple(at + 1 for at in plan.update_catch), first_direct, cross)
        stages(plan.average_lag, plan.average_catch, chunks, average)
        if wide_chunks:

            def wides_done(after):
                return sum((jnp.where(after >= at, n, 0) for at, n in plan.wide_steps), jnp.int32(0))

            def one(m, carry):
                wide_part(m)
                return carry

            lax.fori_loop(wides_done(t - 1), wides_done(t), one, 0)

        return carry

    lax.fori_loop(0, chunks + 5, step, 0)

    for slot in range(SLOTS):
        wait_sent(slot)
        wait_blended(slot)
    wait_bytes(got_e.at[pl.ds(0, e_peers)], e_send)
    if wide_chunks:
        wait_bytes(wide_side, w_send)
    for q in range(wide_chunks):
        for i in range(6):
            wait_bytes(wide_y.at[q, i], wy_send.at[q, i])

    def last_across(q, carry):
        wait_bytes(got_d.at[q], d_send.at[q])
        return carry

    lax.fori_loop(0, plan.direct, last_across, 0)
    if crossing:

        def last_early(b, carry):
            wait_bytes(got_ec.at[b], ec_send.at[b])
            return carry

        def last_cross(k, carry):
            wait_bytes(got_c.at[k], c_send.at[k])
            return carry

        lax.fori_loop(0, row_blocks, last_early, 0)
        lax.fori_loop(0, first_direct, last_cross, 0)

    def last(k, carry):
        wait_bytes(got_f.at[k, pl.ds(0, SIDE - 1)], f_send.at[k])
        for n in range(2):
            wait_bytes(blended.at[0, n, pl.ds(0, SIDE - 1)], b_recv.at[k, n])
        return carry

    lax.fori_loop(0, chunks, last, 0)


def outer_step(plan, arrays):
    acts, weights = arrays[1], arrays[3]
    tokens = acts.shape[0]
    shard, width = weights.shape
    col_blocks, row_blocks = width // CW, shard // ROWS
    chunks = col_blocks * row_blocks
    crossing, wides = max(plan.crossing, 1), max(plan.wide_chunks, 1)
    f32 = jnp.float32
    dma = pltpu.SemaphoreType.DMA
    anywhere = pl.BlockSpec(memory_space=pl.ANY)
    wide = pltpu.VMEM((wides, YS, 2, ROWS, CW // 2), f32)
    return pl.pallas_call(
        functools.partial(kernel, plan),
        out_shape=[jax.ShapeDtypeStruct((shard, width), f32)] * 2,
        in_specs=[pl.BlockSpec(memory_space=pltpu.SMEM)] + [anywhere] * 7,
        out_specs=[anywhere] * 2,
        scratch_shapes=[
            pltpu.VMEM((row_blocks, 2 * YS, tokens, ROWS), jnp.bfloat16),
            pltpu.VMEM((col_blocks, tokens, CW), jnp.bfloat16),
            pltpu.VMEM((5, col_blocks, shard, CW), f32),
            pltpu.VMEM((SLOTS, 8, ROWS, CW), f32),
            pltpu.VMEM((chunks - plan.wide_chunks, 6, ROWS, CW), f32),
            pltpu.VMEM((chunks - plan.wide_chunks, ROWS, CW), f32),
            pltpu.VMEM((chunks, ROWS, CW), f32),
            pltpu.VMEM((chunks, SIDE, PIECE, CW), f32),
            pltpu.VMEM((chunks, crossing, PIECE, CW), f32),
            pltpu.VMEM((chunks, crossing, PIECE, CW), f32),
            pltpu.VMEM((FARMS, PIECE, CW), f32),
            pltpu.VMEM((SLOTS, 2, SIDE, PIECE, CW), f32),
            pltpu.VMEM((plan.direct, SIDE, PIECE, CW), f32),
            pltpu.VMEM((row_blocks, SIDE, PIECE, width), f32),
            pltpu.VMEM((SIDE if plan.crossing else FARMS, row_blocks, PIECE, width), f32),
            pltpu.VMEM((row_blocks, crossing, PIECE, width), f32),
            pltpu.VMEM((row_blocks, crossing, PIECE, width), f32),
            pltpu.VMEM((SIDE + crossing, PIECE, width), f32),
            wide,
            wide,
            wide,
            pltpu.VMEM((wides, 6, ROWS, CW // 2), f32),
            pltpu.SMEM((2 * SIDE + crossing,), jnp.int32),
            dma((row_blocks,)),
            dma((6,)),
            dma((SLOTS, 6)),
            dma((chunks, 6)),
            dma((SLOTS,)),
            dma((chunks,)),
            dma((chunks,)),
            dma((chunks,)),
            dma((chunks,)),
            dma((chunks,)),
            dma((plan.direct,)),
            dma((plan.direct,)),
            dma((SLOTS, 2)),
            dma((chunks, 2)),
            dma((SLOTS, 2)),
            dma,
            dma,
            dma((row_blocks,)),
            dma((row_blocks,)),
            dma,
            dma,
            dma((wides, 6)),
            dma((wides, 6)),
        ],
        compiler_params=pltpu.CompilerParams(
            collective_id=plan.number, has_side_effects=True, vmem_limit_bytes=60 << 20
        ),
        cost_estimate=pl.CostEstimate(
            flops=2 * tokens * 2 * YS * shard * width, bytes_accessed=24 << 20, transcendentals=shard * width
        ),
        name=f"outer_step_{plan.crossing}",
    )(*arrays)


def on_device(activations, out_grads, weights, anchor, adam_m, adam_v, momentum, partner):
    arrays = (partner, activations[0], out_grads[0], weights[0], anchor[0], adam_m[0], adam_v[0], momentum[0])
    c = jnp.sum((partner[:SIDE] >= SIDE).astype(jnp.int32))
    new_momentum, new_anchor = lax.switch((c > 4).astype(jnp.int32) + (c > 6).astype(jnp.int32), (functools.partial(outer_step, Plan(0, 4, 1, 3, ((1, 3), (2, 2), (3, 2), (4, 1), (5, 1), (7, 1), (9, 1), (11, 1)), 3, 4, 3, (), 5, ())), functools.partial(outer_step, Plan(1, 6, 1, 2, ((1, 3), (2, 2), (3, 2), (4, 1)), 3, 4, 3, (), 5, ())), functools.partial(outer_step, Plan(2, 8, 1, 0, (), 3, 4, 3, (), 5, ()))), arrays)
    return new_anchor[None], new_momentum[None]


def solution(mesh):
    split = P("farm", "fsdp", None)
    return jax.shard_map(
        on_device, mesh=mesh, in_specs=(split,) * 7 + (P(),), out_specs=(split, split), check_vma=False
    )
```
